32 devices in a mesh: groups: 2 (over y), feat: 4 (over z), dp: 4 (over x, core).
Axes of the slice: x: 2, y: 2, z: 4, core: 2. Of those that a mesh axis runs over, the one named last changes fastest.
Arguments:
- activations: bfloat16 [12288, 29568], P(('groups', 'dp'), 'feat'), parts along dimension 0, may hold values from -6 to 6
- test_matrix: bfloat16 [29568, 512], P('feat'), may hold values from -6 to 6
Outputs:
- range_sketch: float32 [1024, 29568], P(('groups', 'dp'), 'feat'), parts along dimension 0
- core: float32 [1024, 512], P(('groups', 'dp')), parts along dimension 0
The draws below stay inside these ranges and needn't reach their ends.
There are 2 independent parts, one for each index of `groups`. The reference program is written for one: setup_inputs(seed, part) draws one part's arguments, and reference() takes and returns one part's arrays. A program takes and returns all parts, laid end to end along the dimension named above; an argument that names none is the same for every part. Nothing has to cross between parts.
All inputs are finite; a program needn't handle non-finite values.
Results may differ from the reference program's by a relative error of at most 0.0026.
Values may be sent and summed in bfloat16 or wider, within the bound.
A program may use at most 128 MiB of HBM per device.

```python
import jax
import jax.numpy as jnp
from jax import lax

F = 29568
R = 512
TOKENS = 6144


def levels(key, shape, pieces, low, high):
    loudness = 1.0
    for position, parts in pieces:
        heights = jax.random.uniform(jax.random.fold_in(jax.random.fold_in(key, 6), position), (parts,), jnp.float32, low / len(pieces), high / len(pieces))
        loudness = loudness * jnp.repeat(jnp.exp(heights), shape[position] // parts).reshape((-1,) + (1,) * (len(shape) - 1 - position))
    return loudness


def noise(key, extent, scale, reach, pieces=(), dtype=jnp.bfloat16):
    level = levels(key, extent, pieces, -0.22, 0.18) if pieces else 1.0
    result = jax.random.normal(key, extent, jnp.float32) * scale * level
    return jnp.minimum(jnp.maximum(result, -reach), reach).astype(dtype)


def setup_inputs(seed: int = 0, part: int = 0) -> dict:
    key_list = jax.random.split(jax.random.key(seed), 3)
    part_keys = jax.random.split(jax.random.fold_in(key_list[2], part), 3)
    return {
        "activations": noise(part_keys[0], (TOKENS, F), 1.0, 6.0, ((0, 4), (1, 4))),
        "test_matrix": noise(key_list[1], (F, R), 1.0, 6.0, ((0, 4),)),
    }


def reference(activations, test_matrix):
    sketched = jnp.dot(activations, test_matrix, preferred_element_type=jnp.float32).astype(jnp.bfloat16)
    range_sketch = lax.dot_general(sketched, activations, (((0,), (0,)), ((), ())), preferred_element_type=jnp.float32) * (1.0 / TOKENS)
    core = jnp.dot(range_sketch, test_matrix.astype(jnp.float32), precision=lax.Precision.HIGHEST) * (1.0 / F)
    return (range_sketch, core)
```

```python
import functools

import jax
import jax.numpy as jnp
from jax import lax
from jax.experimental import pallas as pl
from jax.experimental.pallas import tpu as pltpu
from jax.sharding import PartitionSpec as P

F = 29568
MESH = pl.DeviceIdType.MESH
F32, BF16 = jnp.float32, jnp.bfloat16
TB = 256
CB = 512


def plain(activations, test_matrix):
    tokens_here = activations.shape[0]
    inverse_tokens = 1.0 / (tokens_here * lax.axis_size("dp"))
    partial_rows = jnp.dot(activations, test_matrix, preferred_element_type=F32)
    shares = lax.psum_scatter(partial_rows, "feat", scatter_dimension=1, tiled=True).astype(BF16)
    sketched = lax.all_gather(shares, "feat", axis=1, tiled=True)
    product = lax.dot_general(
        sketched, activations, (((0,), (0,)), ((), ())), preferred_element_type=F32
    )
    range_sketch = lax.psum_scatter(product * inverse_tokens, "dp", scatter_dimension=0, tiled=True)
    core_part = jnp.dot(
        range_sketch, test_matrix.astype(F32), precision=lax.Precision.HIGHEST
    ) * (1.0 / F)
    core = lax.psum(core_part, "feat")
    return (range_sketch, core)


def kernel(
    inv_t, inv_core,
    a_hbm, om_hbm, range_ref, core_ref,
    a, om1, om2, st, p1, p2, z1s, z1p, z1t, z2p, z2t,
    ps, pr, qs, qr, keep, xs, xr,
    cpart, cpr, cxs, cxr, cout,
    ld, zs, zr, zs2, zr2, ss, sr, psem, prem, qsem, qrem, xsem, xrem, csem, crem,
):
    T, W = a.shape
    NB = T // TB
    FULL = W // CB
    TAIL = W - FULL * CB
    TAILP = -(-TAIL // 128) * 128

    z = lax.axis_index("feat")
    d = lax.axis_index("dp")
    x, c = d // 2, d % 2
    inner = jnp.logical_and(z >= 1, z <= 2)
    outer = jnp.logical_not(inner)
    hop = jnp.where(inner, 3 * (z - 1), 1 + z // 3)
    hop = jnp.clip(hop, 0, 3)
    mid = jnp.clip(3 - z, 0, 3)
    pair = 2 * x + (1 - c)
    across = 2 * (1 - x) + c

    def rows(ref, s):
        return ref.at[pl.ds(pl.multiple_of(s * TB, TB), TB), :]

    h_other = pl.multiple_of((1 - x) * 256, 256)
    h_own = pl.multiple_of(x * 256, 256)

    ld_om1 = pltpu.make_async_copy(om_hbm.at[:, pl.ds(h_other, 256)], om1, ld.at[NB])
    ld_om2 = pltpu.make_async_copy(om_hbm.at[:, pl.ds(h_own, 256)], om2, ld.at[NB + 1])

    def ld_a(s):
        return pltpu.make_async_copy(rows(a_hbm, s), rows(a, s), ld.at[s])

    ld_om1.start()
    ld_a(0).start()
    ld_om2.start()
    for s in range(1, NB):
        ld_a(s).start()

    barrier = pltpu.get_barrier_semaphore()
    for k in range(1, 4):
        pl.semaphore_signal(barrier, inc=1, device_id={"feat": lax.rem(z + k, 4)}, device_id_type=MESH)
    for other in (pair, across):
        pl.semaphore_signal(barrier, inc=1, device_id={"dp": other}, device_id_type=MESH)
    pl.semaphore_wait(barrier, 5)

    def rcopy(src, dst, s1, s2, dev):
        return pltpu.make_async_remote_copy(
            src_ref=src, dst_ref=dst, send_sem=s1, recv_sem=s2, device_id=dev, device_id_type=MESH
        )

    def first_p(s):
        return rcopy(rows(z1s, s), rows(z1p, s), zs.at[0, s], zr.at[0, s], {"feat": hop})

    def first_t(s):
        return rcopy(rows(z1s, s), rows(z1t, s), zs.at[1, s], zr.at[1, s], {"feat": mid})

    def second_p(s):
        return rcopy(rows(p2, s), rows(z2p, s), zs2.at[0, s], zr2.at[0, s], {"feat": hop})

    def second_t(s):
        return rcopy(rows(p2, s), rows(z2t, s), zs2.at[1, s], zr2.at[1, s], {"feat": mid})

    def st_at(h, s):
        return st.at[pl.ds(h, 256), pl.ds(pl.multiple_of(s * TB, TB), TB)]

    def send_s(half, h, s):
        return rcopy(st_at(h, s), st_at(h, s), ss.at[half, s], sr.at[half, s], {"feat": hop})

    ld_om1.wait()

    @pl.loop(0, NB + 2)
    def _(s):
        @pl.when(s < NB)
        def _():
            ld_a(s).wait()
            part = jnp.dot(rows(a, s)[...], om1[...], preferred_element_type=F32)

            @pl.when(outer)
            def _():
                rows(z1s, s)[...] = part.astype(BF16)
                first_p(s).start()

            @pl.when(inner)
            def _():
                rows(p1, s)[...] = part

        @pl.when(jnp.logical_and(inner, jnp.logical_and(s >= 1, s <= NB)))
        def _():
            k = s - 1
            first_p(k).wait_recv()
            total = rows(p1, k)[...] + rows(z1p, k)[...].astype(F32)
            rows(p1, k)[...] = total
            rows(z1s, k)[...] = total.astype(BF16)
            first_t(k).start()

        @pl.when(s == 0)
        def _():
            ld_om2.wait()

        @pl.when(s < NB)
        def _():
            rows(p2, s)[...] = jnp.dot(rows(a, s)[...], om2[...], preferred_element_type=F32)

        @pl.when(jnp.logical_and(inner, s >= 2))
        def _():
            k = s - 2
            first_t(k).wait_recv()
            total = rows(p1, k)[...] + rows(z1t, k)[...].astype(F32)
            st_at(h_other, k)[...] = total.T.astype(BF16)
            send_s(0, h_other, k).start()

    @pl.when(outer)
    def _():
        @pl.loop(0, NB)
        def _(s):
            second_p(s).start()

        @pl.loop(0, NB)
        def _(s):
            send_s(0, h_other, s).wait_recv()

    if TAIL:
        for buf in (ps, qs, xs):
            buf[FULL] = jnp.zeros(buf.shape[1:], BF16)

    def span(j, width):
        return pl.ds(j * CB, width) if isinstance(j, int) else pl.ds(pl.multiple_of(j * CB, CB), width)

    def pcopy(j, wp):
        view = lambda r: r.at[j, :, pl.ds(0, wp)]
        return rcopy(view(ps), view(pr), psem.at[j], prem.at[j], {"dp": pair})

    def qcopy(j, wp):
        view = lambda r: r.at[j, :, pl.ds(0, wp)]
        return rcopy(view(qs), view(qr), qsem.at[j], qrem.at[j], {"dp": pair})

    def xcopy(j, wp):
        view = lambda r: r.at[j, :, pl.ds(0, wp)]
        return rcopy(view(xs), view(xr), xsem.at[j], xrem.at[j], {"dp": across})

    mine = pl.multiple_of(c * 128, 128)
    theirs = pl.multiple_of((1 - c) * 128, 128)

    def product(h, base, j, width):
        return jnp.dot(st[pl.ds(h + base, 128), :], a[:, span(j, width)], preferred_element_type=F32)

    def multiply(h, j, width, wp, out, copy):
        out[j, :, pl.ds(0, width)] = product(h, theirs, j, width).astype(BF16)
        copy(j, wp).start()
        keep[lax.rem(j, 2), :, pl.ds(0, width)] = product(h, mine, j, width)

    def combine_x(j, width, wp):
        pcopy(j, wp).wait_recv()
        total = keep[lax.rem(j, 2), :, pl.ds(0, width)] + pr[j, :, pl.ds(0, width)].astype(F32)
        xs[j, :, pl.ds(0, width)] = total.astype(BF16)
        xcopy(j, wp).start()

    def combine_out(j, width, wp):
        qcopy(j, wp).wait_recv()
        xcopy(j, wp).wait_recv()
        total = keep[lax.rem(j, 2), :, pl.ds(0, width)] + qr[j, :, pl.ds(0, width)].astype(F32)
        total = total + xr[j, :, pl.ds(0, width)].astype(F32)
        range_ref[:, span(j, width)] = total * inv_t

    def sweep(h, out, copy, combine):
        multiply(h, 0, CB, CB, out, copy)

        @pl.loop(1, FULL)
        def _(j):
            multiply(h, j, CB, CB, out, copy)
            combine(j - 1, CB, CB)

        if TAIL:
            multiply(h, FULL, TAIL, TAILP, out, copy)
        combine(FULL - 1, CB, CB)
        if TAIL:
            combine(FULL, TAIL, TAILP)

    sweep(h_other, ps, pcopy, combine_x)

    @pl.when(inner)
    def _():
        @pl.loop(0, NB + 1)
        def _(s):
            @pl.when(s < NB)
            def _():
                second_p(s).wait_recv()
                rows(p2, s)[...] = rows(p2, s)[...] + rows(z2p, s)[...]
                second_t(s).start()

            @pl.when(s >= 1)
            def _():
                k = s - 1
                second_t(k).wait_recv()
                total = rows(p2, k)[...] + rows(z2t, k)[...]
                st_at(h_own, k)[...] = total.T.astype(BF16)
                send_s(1, h_own, k).start()

    @pl.when(outer)
    def _():
        @pl.loop(0, NB)
        def _(s):
            send_s(1, h_own, s).wait_recv()

    cols = st[pl.ds(pl.multiple_of(z * 128, 128), 128), :]
    for q in range(4):
        cpart[q] = lax.dot_general(
            st[pl.ds(q * 128, 128), :], cols, (((1,), (1,)), ((), ())), preferred_element_type=F32
        )

    def cpair(k):
        owner = 2 * ((1 - x) if k == 0 else x)
        return rcopy(cpart.at[owner + 1 - c], cpr.at[k], csem.at[k], crem.at[k], {"dp": pair})

    cpair(0).start()
    cpair(1).start()
    cross = rcopy(cxs, cxr, csem.at[2], crem.at[2], {"dp": across})
    cpair(0).wait_recv()
    cxs[...] = cpart[2 * (1 - x) + c] + cpr[0]
    cross.start()

    def ccopy(k):
        return rcopy(cout.at[0], cout.at[k], csem.at[2 + k], crem.at[2 + k], {"feat": lax.rem(z + k, 4)})

    def finish_core():
        cpair(1).wait_recv()
        cross.wait_recv()
        cout[0] = (cpart[2 * x + c] + cpr[1] + cxr[...]) * inv_core
        for k in range(1, 4):
            ccopy(k).start()

    finish_core()
    sweep(h_own, qs, qcopy, combine_out)

    for k in range(1, 4):
        ccopy(k).wait_recv()
    for k in range(4):
        at = pl.multiple_of(lax.rem(z - k + 4, 4) * 128, 128)
        core_ref[:, pl.ds(at, 128)] = cout[k]

    cpair(0).wait_send()
    cpair(1).wait_send()
    cross.wait_send()
    for k in range(1, 4):
        ccopy(k).wait_send()

    @pl.loop(0, NB)
    def _(s):
        @pl.when(outer)
        def _():
            first_p(s).wait_send()
            second_p(s).wait_send()

        @pl.when(inner)
        def _():
            first_t(s).wait_send()
            second_t(s).wait_send()
            send_s(0, h_other, s).wait_send()
            send_s(1, h_own, s).wait_send()

    def drain(j, wp):
        pcopy(j, wp).wait_send()
        qcopy(j, wp).wait_send()
        xcopy(j, wp).wait_send()

    @pl.loop(0, FULL)
    def _(j):
        drain(j, CB)

    if TAIL:
        drain(FULL, TAILP)


def fused(activations, test_matrix):
    T, W = activations.shape
    R = test_matrix.shape[1]
    NB = T // TB
    NC = -(-W // CB)
    tokens = T * lax.axis_size("dp")
    units = W * lax.axis_size("feat")
    DMA = pltpu.SemaphoreType.DMA
    V = pltpu.VMEM
    return pl.pallas_call(
        functools.partial(kernel, 1.0 / tokens, 1.0 / tokens / units),
        out_shape=(
            jax.ShapeDtypeStruct((R // 4, W), F32),
            jax.ShapeDtypeStruct((R // 4, R), F32),
        ),
        in_specs=[pl.BlockSpec(memory_space=pl.ANY)] * 2,
        out_specs=(pl.BlockSpec(memory_space=pltpu.VMEM),) * 2,
        scratch_shapes=[
            V((T, W), BF16), V((W, 256), BF16), V((W, 256), BF16), V((R, T), BF16),
            V((T, 256), F32), V((T, 256), F32),
            V((T, 256), BF16), V((T, 256), BF16), V((T, 256), BF16),
            V((T, 256), F32), V((T, 256), F32),
            V((NC, 128, CB), BF16), V((NC, 128, CB), BF16), V((NC, 128, CB), BF16), V((NC, 128, CB), BF16),
            V((2, 128, CB), F32),
            V((NC, 128, CB), BF16), V((NC, 128, CB), BF16),
            V((4, 128, 128), F32), V((2, 128, 128), F32), V((128, 128), F32), V((128, 128), F32),
            V((4, 128, 128), F32),
            DMA((NB + 2,)), DMA((2, NB)), DMA((2, NB)), DMA((2, NB)), DMA((2, NB)), DMA((2, NB)), DMA((2, NB)),
            DMA((NC,)), DMA((NC,)), DMA((NC,)), DMA((NC,)), DMA((NC,)), DMA((NC,)),
            DMA((6,)), DMA((6,)),
        ],
        compiler_params=pltpu.CompilerParams(
            collective_id=0, has_side_effects=True, vmem_limit_bytes=63 * 1024 * 1024
        ),
        cost_estimate=pl.CostEstimate(
            flops=4 * T * W * R, bytes_accessed=2 * T * W + 4 * W * R, transcendentals=0
        ),
    )(activations, test_matrix)


def solution(mesh):
    placed = (P(("groups", "dp"), "feat"), P("feat", None))

    def body(activations, test_matrix):
        T, W = activations.shape
        fits = (
            mesh.shape["feat"] == 4
            and mesh.shape["dp"] == 4
            and test_matrix.shape[1] == 512
            and T % TB == 0
            and W % 16 == 0
            and 2 * CB <= W <= 7424
            and T <= 1536
        )
        return (fused if fits else plain)(activations, test_matrix)

    return jax.shard_map(
        body,
        mesh=mesh,
        in_specs=placed,
        out_specs=(P(("groups", "dp"), "feat"), P(("groups", "dp"), None)),
        check_vma=False,
    )
```

```python
import functools

import jax
import jax.numpy as jnp
from jax import lax
from jax.experimental import pallas as pl
from jax.experimental.pallas import tpu as pltpu
from jax.sharding import PartitionSpec as P

F = 29568
MESH = pl.DeviceIdType.MESH
F32, BF16 = jnp.float32, jnp.bfloat16
TB = 256
CB = 512


def plain(activations, test_matrix):
    tokens_here = activations.shape[0]
    inverse_tokens = 1.0 / (tokens_here * lax.axis_size("dp"))
    partial_rows = jnp.dot(activations, test_matrix, preferred_element_type=F32)
    shares = lax.psum_scatter(partial_rows, "feat", scatter_dimension=1, tiled=True).astype(BF16)
    sketched = lax.all_gather(shares, "feat", axis=1, tiled=True)
    product = lax.dot_general(
        sketched, activations, (((0,), (0,)), ((), ())), preferred_element_type=F32
    )
    range_sketch = lax.psum_scatter(product * inverse_tokens, "dp", scatter_dimension=0, tiled=True)
    core_part = jnp.dot(
        range_sketch, test_matrix.astype(F32), precision=lax.Precision.HIGHEST
    ) * (1.0 / F)
    core = lax.psum(core_part, "feat")
    return (range_sketch, core)


def kernel(
    inv_core,
    a_hbm, om_hbm, range_ref, core_ref,
    a, om, omt, st, p1, p2, z1s, z1p, z1t, z2p, z2t,
    ps, pr, qs, qr, keep, xs, xr,
    cpart, cpr, cxs, cxr, cout,
    ld, lo, zs, zr, zs2, zr2, ss, sr, psem, prem, qsem, qrem, xsem, xrem, csem, crem,
):
    W, T = a.shape
    NB = T // TB
    FULL = W // CB
    TAIL = W - FULL * CB

    z = lax.axis_index("feat")
    d = lax.axis_index("dp")
    x, c = d // 2, d % 2
    inner = jnp.logical_and(z >= 1, z <= 2)
    outer = jnp.logical_not(inner)
    hop = jnp.where(inner, 3 * (z - 1), 1 + z // 3)
    hop = jnp.clip(hop, 0, 3)
    mid = jnp.clip(3 - z, 0, 3)
    pair = 2 * x + (1 - c)
    across = 2 * (1 - x) + c

    def ld_om(half):
        chip = (1 - x) if half == 0 else x
        return [
            pltpu.make_async_copy(
                om_hbm.at[:, pl.ds(pl.multiple_of((2 * chip + core) * 128, 128), 128)],
                om.at[:, pl.ds(at, 128)],
                lo.at[half, at // 128],
            )
            for at, core in ((0, c), (128, 1 - c))
        ]

    def lanes(ref, s):
        return ref.at[:, pl.ds(pl.multiple_of(s * TB, TB), TB)]

    def ld_a(s):
        return pltpu.make_async_copy(lanes(a_hbm, s), lanes(a, s), ld.at[s])

    for copy in ld_om(0):
        copy.start()
    for s in range(2):
        ld_a(s).start()

    barrier = pltpu.get_barrier_semaphore()
    for k in range(1, 4):
        pl.semaphore_signal(barrier, inc=1, device_id={"feat": lax.rem(z + k, 4)}, device_id_type=MESH)
    for other in (pair, across):
        pl.semaphore_signal(barrier, inc=1, device_id={"dp": other}, device_id_type=MESH)
    pl.semaphore_wait(barrier, 5)

    def rcopy(src, dst, s1, s2, dev):
        return pltpu.make_async_remote_copy(
            src_ref=src, dst_ref=dst, send_sem=s1, recv_sem=s2, device_id=dev, device_id_type=MESH
        )

    def first_p(s, u):
        view = lambda r: r.at[s, pl.ds(128 * u, 128), :]
        return rcopy(view(z1s), view(z1p), zs.at[0, 2 * s + u], zr.at[0, 2 * s + u], {"feat": hop})

    def first_t(s, u):
        view = lambda r: r.at[s, pl.ds(128 * u, 128), :]
        return rcopy(view(z1s), view(z1t), zs.at[1, 2 * s + u], zr.at[1, 2 * s + u], {"feat": mid})

    def first_s(s, u):
        view = st.at[0, pl.ds(pl.multiple_of(s * TB, TB), TB), pl.ds(128 * u, 128)]
        return rcopy(view, view, ss.at[0, 2 * s + u], sr.at[0, 2 * s + u], {"feat": hop})

    def second_p(k):
        return rcopy(p2.at[k], z2p.at[k], zs2.at[0, k], zr2.at[0, k], {"feat": hop})

    def second_t(k):
        return rcopy(p2.at[k], z2t.at[k], zs2.at[1, k], zr2.at[1, k], {"feat": mid})

    def st_at(k):
        rows = pl.ds(pl.multiple_of(lax.rem(k, NB) * TB, TB), TB)
        return st.at[1, rows, pl.ds(pl.multiple_of(jnp.where(k < NB, 128, 0), 128), 128)]

    def second_s(k):
        return rcopy(st_at(k), st_at(k), ss.at[1, k], sr.at[1, k], {"feat": hop})

    def turn(half):
        for copy in ld_om(half):
            copy.wait()

        @pl.loop(0, W // 256)
        def _(k):
            at = pl.ds(pl.multiple_of(k * 256, 256), 256)
            omt[half, :, at] = om[at, :].T

        done = W // 256 * 256
        if W > done:
            omt[half, :, pl.ds(done, W - done)] = om[pl.ds(done, W - done), :].T

    turn(0)
    for copy in ld_om(1):
        copy.start()

    @pl.loop(0, NB + 2)
    def _(s):
        @pl.when(s < NB)
        def _():
            ld_a(s).wait()

            @pl.when(s + 2 < NB)
            def _():
                ld_a(s + 2).start()

            part = jnp.dot(omt[0], lanes(a, s)[...], preferred_element_type=F32)

            @pl.when(outer)
            def _():
                z1s[s] = part.astype(BF16)
                first_p(s, 0).start()
                first_p(s, 1).start()

            @pl.when(inner)
            def _():
                p1[s] = part

        @pl.when(jnp.logical_and(inner, jnp.logical_and(s >= 1, s <= NB)))
        def _():
            k = s - 1
            for u in range(2):
                ranks = pl.ds(128 * u, 128)
                first_p(k, u).wait_recv()
                total = p1[k, ranks, :] + z1p[k, ranks, :].astype(F32)
                p1[k, ranks, :] = total
                z1s[k, ranks, :] = total.astype(BF16)
                first_t(k, u).start()

        @pl.when(s == 0)
        def _():
            turn(1)

        @pl.when(s < NB)
        def _():
            part = jnp.dot(omt[1], lanes(a, s)[...], preferred_element_type=F32)
            p2[s] = part[128:]
            p2[NB + s] = part[:128]

        @pl.when(jnp.logical_and(inner, s >= 2))
        def _():
            k = s - 2
            for u in range(2):
                ranks = pl.ds(128 * u, 128)
                first_t(k, u).wait_recv()
                total = p1[k, ranks, :] + z1t[k, ranks, :].astype(F32)
                st[0, pl.ds(pl.multiple_of(k * TB, TB), TB), ranks] = total.T.astype(BF16)
                first_s(k, u).start()

    @pl.when(outer)
    def _():
        @pl.loop(0, 2 * NB)
        def _(k):
            second_p(k).start()

        @pl.loop(0, NB)
        def _(s):
            first_s(s, 0).wait_recv()
            first_s(s, 1).wait_recv()

    def span(j, width):
        return pl.ds(j * CB, width) if isinstance(j, int) else pl.ds(pl.multiple_of(j * CB, CB), width)

    def pcopy(j, width):
        view = lambda r: r.at[j, pl.ds(0, width), :]
        return rcopy(view(ps), view(pr), psem.at[j], prem.at[j], {"dp": pair})

    def qcopy(j, width):
        view = lambda r: r.at[j, pl.ds(0, width), :]
        return rcopy(view(qs), view(qr), qsem.at[j], qrem.at[j], {"dp": pair})

    def xcopy(j, width):
        view = lambda r: r.at[j, pl.ds(0, width), :]
        return rcopy(view(xs), view(xr), xsem.at[j], xrem.at[j], {"dp": across})

    def multiply_x(j, width):
        block = jnp.dot(a[span(j, width), :], st[0], preferred_element_type=F32)
        ps[j, pl.ds(0, width), :] = block[:, 128:].astype(BF16)
        pcopy(j, width).start()
        keep[lax.rem(j, 2), pl.ds(0, width), :] = block[:, :128]

    def combine_x(j, width):
        pcopy(j, width).wait_recv()
        total = keep[lax.rem(j, 2), pl.ds(0, width), :] + pr[j, pl.ds(0, width), :].astype(F32)
        xs[j, pl.ds(0, width), :] = total.astype(BF16)
        xcopy(j, width).start()

    multiply_x(0, CB)

    @pl.loop(1, FULL)
    def _(j):
        multiply_x(j, CB)
        combine_x(j - 1, CB)

    if TAIL:
        multiply_x(FULL, TAIL)
    combine_x(FULL - 1, CB)
    if TAIL:
        combine_x(FULL, TAIL)

    def second_step(t):
        @pl.when(t < 2 * NB)
        def _():
            second_p(t).wait_recv()
            p2[t] = p2[t] + z2p[t]
            second_t(t).start()

        @pl.when(t >= 1)
        def _():
            k = t - 1
            second_t(k).wait_recv()
            total = p2[k] + z2t[k]
            st_at(k)[...] = total.T.astype(BF16)
            second_s(k).start()

    @pl.when(inner)
    def _():
        @pl.loop(0, NB + 1)
        def _(t):
            second_step(t)

    @pl.when(outer)
    def _():
        @pl.loop(0, NB)
        def _(k):
            second_s(k).wait_recv()

    def multiply_q(j, width):
        block = jnp.dot(a[span(j, width), :], st[1, :, pl.ds(128, 128)], preferred_element_type=F32)
        qs[j, pl.ds(0, width), :] = block.astype(BF16)
        qcopy(j, width).start()

    within = min(FULL // 2, NB)

    @pl.loop(0, FULL)
    def _(j):
        multiply_q(j, CB)

        @pl.when(jnp.logical_and(inner, jnp.logical_and(lax.rem(j, 2) == 1, j // 2 < within)))
        def _():
            second_step(NB + 1 + j // 2)

    if TAIL:
        multiply_q(FULL, TAIL)

    @pl.when(inner)
    def _():
        @pl.loop(NB + 1 + within, 2 * NB + 1)
        def _(t):
            second_step(t)

    @pl.when(outer)
    def _():
        @pl.loop(NB, 2 * NB)
        def _(k):
            second_s(k).wait_recv()

    near = jnp.where(z // 2 == x, 1, 0)
    at = pl.multiple_of(jnp.where(z % 2 == c, 0, 128), 128)
    cols = st[near, :, pl.ds(at, 128)]
    for half in range(2):
        both = lax.dot_general(st[half], cols, (((0,), (0,)), ((), ())), preferred_element_type=F32)
        cpart[half, 0] = both[:128]
        cpart[half, 1] = both[128:]

    def cpair(half):
        return rcopy(cpart.at[half, 1], cpr.at[half], csem.at[half], crem.at[half], {"dp": pair})

    cpair(0).start()
    cpair(1).start()
    cross = rcopy(cxs, cxr, csem.at[2], crem.at[2], {"dp": across})

    def ccopy(k):
        return rcopy(cout.at[0], cout.at[k], csem.at[2 + k], crem.at[2 + k], {"feat": lax.rem(z + k, 4)})

    def finish(j, width):
        total = jnp.dot(a[span(j, width), :], st[1, :, pl.ds(0, 128)], preferred_element_type=F32)
        qcopy(j, width).wait_recv()
        total = total + qr[j, pl.ds(0, width), :].astype(F32)
        xcopy(j, width).wait_recv()
        range_ref[span(j, width), :] = total + xr[j, pl.ds(0, width), :].astype(F32)

    @pl.loop(0, FULL)
    def _(j):
        @pl.when(j == 2)
        def _():
            cpair(0).wait_recv()
            cxs[...] = cpart[0, 0] + cpr[0]
            cross.start()

        finish(j, CB)

    cpair(1).wait_recv()
    cross.wait_recv()
    cout[0] = (cpart[1, 0] + cpr[1] + cxr[...]) * inv_core
    for k in range(1, 4):
        ccopy(k).start()
    if TAIL:
        finish(FULL, TAIL)

    for k in range(1, 4):
        ccopy(k).wait_recv()
    for k in range(4):
        at = pl.multiple_of(lax.rem(z - k + 4, 4) * 128, 128)
        core_ref[:, pl.ds(at, 128)] = cout[k]

    cpair(0).wait_send()
    cpair(1).wait_send()
    cross.wait_send()
    for k in range(1, 4):
        ccopy(k).wait_send()

    @pl.loop(0, NB)
    def _(s):
        @pl.when(outer)
        def _():
            for u in range(2):
                first_p(s, u).wait_send()
                second_p(NB * u + s).wait_send()

        @pl.when(inner)
        def _():
            for u in range(2):
                first_t(s, u).wait_send()
                first_s(s, u).wait_send()
                second_t(NB * u + s).wait_send()
                second_s(NB * u + s).wait_send()

    def drain(j, width):
        pcopy(j, width).wait_send()
        qcopy(j, width).wait_send()
        xcopy(j, width).wait_send()

    @pl.loop(0, FULL)
    def _(j):
        drain(j, CB)

    if TAIL:
        drain(FULL, TAIL)


def fused(activations, test_matrix):
    T, W = activations.shape
    R = test_matrix.shape[1]
    NB = T // TB
    NC = -(-W // CB)
    tokens = T * lax.axis_size("dp")
    units = W * lax.axis_size("feat")
    DMA = pltpu.SemaphoreType.DMA
    V = pltpu.VMEM
    by_unit, core = pl.pallas_call(
        functools.partial(kernel, 1.0 / tokens / units),
        out_shape=(
            jax.ShapeDtypeStruct((W, R // 4), F32),
            jax.ShapeDtypeStruct((R // 4, R), F32),
        ),
        in_specs=[pl.BlockSpec(memory_space=pl.ANY)] * 2,
        out_specs=(pl.BlockSpec(memory_space=pltpu.VMEM),) * 2,
        scratch_shapes=[
            V((W, T), BF16), V((W, 256), BF16), V((2, 256, W), BF16), V((2, T, 256), BF16),
            V((NB, 256, TB), F32), V((2 * NB, 128, TB), F32),
            V((NB, 256, TB), BF16), V((NB, 256, TB), BF16), V((NB, 256, TB), BF16),
            V((2 * NB, 128, TB), F32), V((2 * NB, 128, TB), F32),
            V((NC, CB, 128), BF16), V((NC, CB, 128), BF16), V((NC, CB, 128), BF16), V((NC, CB, 128), BF16),
            V((2, CB, 128), F32),
            V((NC, CB, 128), BF16), V((NC, CB, 128), BF16),
            V((2, 2, 128, 128), F32), V((2, 128, 128), F32), V((128, 128), F32), V((128, 128), F32),
            V((4, 128, 128), F32),
            DMA((NB,)), DMA((2, 2)),
            DMA((2, 2 * NB)), DMA((2, 2 * NB)), DMA((2, 2 * NB)), DMA((2, 2 * NB)), DMA((2, 2 * NB)), DMA((2, 2 * NB)),
            DMA((NC,)), DMA((NC,)), DMA((NC,)), DMA((NC,)), DMA((NC,)), DMA((NC,)),
            DMA((6,)), DMA((6,)),
        ],
        compiler_params=pltpu.CompilerParams(
            collective_id=0, has_side_effects=True, vmem_limit_bytes=63 * 1024 * 1024
        ),
        cost_estimate=pl.CostEstimate(
            flops=4 * T * W * R, bytes_accessed=2 * T * W + 4 * W * R, transcendentals=0
        ),
    )(activations.T, test_matrix)
    return by_unit.T * (1.0 / tokens), core


def solution(mesh):
    placed = (P(("groups", "dp"), "feat"), P("feat", None))

    def body(activations, test_matrix):
        T, W = activations.shape
        fits = (
            mesh.shape["feat"] == 4
            and mesh.shape["dp"] == 4
            and test_matrix.shape[1] == 512
            and T % TB == 0
            and W % 16 == 0
            and 2 * CB <= W <= 7424
            and T <= 1536
        )
        return (fused if fits else plain)(activations, test_matrix)

    return jax.shard_map(
        body,
        mesh=mesh,
        in_specs=placed,
        out_specs=(P(("groups", "dp"), "feat"), P(("groups", "dp"), None)),
        check_vma=False,
    )
```
